128 devices in a mesh: grp: 8 (over z_hi, x), mem: 16 (over z_lo, y, core).
Axes of the slice: x: 4, y: 4, z: 4 (z_hi: 2, z_lo: 2; z = z_hi * 2 + z_lo), core: 2. Of those that a mesh axis runs over, the one named last changes fastest.
Arguments:
- amplitudes: float32 [16384, 16384], P(('grp', 'mem')), may hold values from -6 to 6
- factors: float32 [16384, 1536], P('mem'), may hold values from -0.046875 to 0.046875
Outputs:
- cycle_term: float32 [16384, 16384], P(('grp', 'mem'))
The draws below stay inside these ranges and needn't reach their ends.
All inputs are finite; a program needn't handle non-finite values.
Results may differ from the reference program's by a relative error of at most 0.000071.
Values sent between devices are 32-bit elements; how exact they have to be, the bound alone decides.
No kernel may reach another device: no remote copies, remote signals or barrier semaphores. Data moves between devices by JAX's collectives and lax.ppermute only.
A program may use at most 128 MiB of HBM per device.

```python
import jax
import jax.numpy as jnp
from jax import lax

NAUX = 1536
NPAIR = 16384


def levels(rng, dims, cuts, low, top_value):
    def one(dim, shards_of):
        heights = jax.random.uniform(jax.random.fold_in(jax.random.fold_in(rng, 6), dim), (shards_of,), jnp.float32, low / len(cuts), top_value / len(cuts))
        return jnp.repeat(jnp.exp(heights), dims[dim] // shards_of).reshape((-1,) + (1,) * (len(dims) - dim - 1))

    factor_of = one(*cuts[0])
    for cut in cuts[1:]:
        factor_of = factor_of * one(*cut)
    return factor_of


def noise(rng, shape, width, reach, split=(), kind=jnp.bfloat16):
    loudness = levels(rng, shape, split, -0.22, 0.18) if split else 1.0
    entries = jax.random.normal(rng, shape, jnp.float32) * width * loudness
    return jnp.minimum(jnp.maximum(entries, -reach), reach).astype(kind)


def setup_inputs(seed: int = 0) -> dict:
    key_list = jax.random.split(jax.random.key(seed), 3)
    return {
        "amplitudes": noise(key_list[0], (NPAIR, NPAIR), 1.0, 6.0, ((0, 128),), jnp.float32),
        "factors": noise(key_list[1], (NPAIR, NAUX), NPAIR ** -0.5, 0.046875, ((0, 16),), jnp.float32),
    }


def reference(amplitudes, factors):
    fitted = jnp.dot(amplitudes, factors, precision=lax.Precision.HIGHEST, preferred_element_type=jnp.float32)
    cycle = jnp.dot(fitted, factors.T, precision=lax.Precision.HIGHEST, preferred_element_type=jnp.float32)
    return cycle + cycle.T
```

```python
import functools

import jax
import jax.numpy as jnp
import numpy as np
from jax import lax
from jax.experimental import pallas as pl
from jax.experimental.pallas import tpu as pltpu
from jax.sharding import Mesh
from jax.sharding import PartitionSpec as P

SIZES = (2, 4, 2, 4, 2)
ALL = ("zh", "x", "zl", "y", "c")
MEM = ("zl", "y", "c")


def permutation(move):
    pairs = []
    for source in range(int(np.prod(SIZES))):
        zh, x, zl, y, c = (int(i) for i in np.unravel_index(source, SIZES))
        tx, ty, tz, tc = move(x, y, 2 * zh + zl, c)
        tx, ty, tz, tc = tx % 4, ty % 4, tz % 4, tc % 2
        pairs.append((source, int(np.ravel_multi_index((tz // 2, tx, tz % 2, ty, tc), SIZES))))
    return pairs


ALONG_X = permutation(lambda x, y, z, c: (x + 1 - 2 * c, y, z, c))
ALONG_Y = permutation(lambda x, y, z, c: (x, y + 1 - 2 * c, z, c))
ALONG_Z = permutation(lambda x, y, z, c: (x, y, z + 1 - 2 * c, c))
CORES = permutation(lambda x, y, z, c: (x, y, z, c + 1))

ROUNDS = (
    ((ALONG_Y, "a00", "a01"), (ALONG_Z, "a00", "a10")),
    ((ALONG_X, "a01", "b01"), (ALONG_Y, "a01", "a02"), (ALONG_Z, "b00", "b10")),
    ((ALONG_X, "a02", "b02"), (ALONG_Y, "a02", "a03"), (ALONG_Z, "a01", "a11")),
    ((ALONG_X, "a03", "b03"), (ALONG_Y, "b10", "b11"), (ALONG_Z, "a03", "a13")),
    ((ALONG_X, "a13", "b13"), (ALONG_Y, "b11", "b12"), (ALONG_Z, "a02", "a12")),
)


PIECES = ["a00", "b00"] + [target for moves in ROUNDS for _, _, target in moves]
SLOTS = 3
NT = (((1,), (1,)), ((), ()))


def dot(a, b):
    return jnp.dot(a, b, precision=lax.Precision.HIGH, preferred_element_type=jnp.float32)


def parts(value):
    high = value.astype(jnp.bfloat16)
    return high, (value - high.astype(jnp.float32)).astype(jnp.bfloat16)


def cycle_kernel(
    rows, mine_at, theirs_at, fitted, *refs
):
    pieces, (owned, other, high, low, held, tiles, in_sems, out_sems) = refs[:-8], refs[-8:]
    count = len(pieces)
    half = pieces[0].shape[0]
    width = min(2 * rows, half)
    per_step = width // rows
    steps = half // width
    high[...], low[...] = parts(fitted[...])

    def fetch(i):
        return pltpu.make_async_copy(pieces[i], held.at[i % SLOTS], in_sems.at[i % SLOTS])

    def drain(i):
        at = pl.ds(mine_at[i], half // rows)
        there = pl.ds(theirs_at[i], half // rows)
        slot = i % 2
        return (
            pltpu.make_async_copy(tiles.at[slot, 0], owned.at[at], out_sems.at[slot, 0]),
            pltpu.make_async_copy(tiles.at[slot, 1], other.at[there], out_sems.at[slot, 1]),
        )

    for i in range(min(SLOTS - 1, count)):
        fetch(i).start()
    for i in range(count):
        if i + SLOTS - 1 < count:
            fetch(i + SLOTS - 1).start()
        fetch(i).wait()
        if i >= 2:
            for copy in drain(i - 2):
                copy.wait()
        for step in range(steps):
            piece_high, piece_low = parts(held[i % SLOTS, step * width : (step + 1) * width])
            product = functools.partial(
                lax.dot_general, dimension_numbers=NT, preferred_element_type=jnp.float32
            )
            total = (
                product(low[...], piece_high) + product(high[...], piece_low)
            ) + product(high[...], piece_high)
            for k in range(per_step):
                for who in range(2):
                    tiles[i % 2, who, step * per_step + k] = total[
                        who * rows : (who + 1) * rows, k * rows : (k + 1) * rows
                    ]
        for copy in drain(i):
            copy.start()
    for i in range(max(count - 2, 0), count):
        for copy in drain(i):
            copy.wait()


def make_cycle(rows, mine_at, theirs_at, fitted, pieces):
    half, depth = pieces[0].shape
    total = len(pieces) * half // rows
    flops = 3 * 2 * fitted.shape[0] * half * depth * len(pieces)
    smem = pl.BlockSpec(memory_space=pltpu.SMEM)
    anywhere = pl.BlockSpec(memory_space=pl.ANY)
    return pl.pallas_call(
        functools.partial(cycle_kernel, rows),
        out_shape=(
            jax.ShapeDtypeStruct((2 * total, rows, rows), jnp.float32),
            jax.ShapeDtypeStruct((total, rows, rows), jnp.float32),
        ),
        in_specs=[smem, smem, pl.BlockSpec(memory_space=pltpu.VMEM)] + [anywhere] * len(pieces),
        out_specs=(anywhere, anywhere),
        scratch_shapes=[
            pltpu.VMEM(fitted.shape, jnp.bfloat16),
            pltpu.VMEM(fitted.shape, jnp.bfloat16),
            pltpu.VMEM((SLOTS, half, depth), jnp.float32),
            pltpu.VMEM((2, 2, half // rows, rows, rows), jnp.float32),
            pltpu.SemaphoreType.DMA((SLOTS,)),
            pltpu.SemaphoreType.DMA((2, 2)),
        ],
        cost_estimate=pl.CostEstimate(
            flops=flops, bytes_accessed=4 * len(pieces) * half * (depth + 2 * rows), transcendentals=0
        ),
        compiler_params=pltpu.CompilerParams(vmem_limit_bytes=40 * 2**20),
        name="cycle",
    )(mine_at, theirs_at, fitted, *pieces)


def join_kernel(straight, mirrored, out):
    rows = straight.shape[1]
    for k in range(straight.shape[0]):
        out[:, k * rows : (k + 1) * rows] = straight[k] + mirrored[k].T


def join(straight, mirrored):
    count, rows, _ = straight.shape
    group = 16
    tile = pl.BlockSpec((group, rows, rows), lambda i: (i, 0, 0))
    return pl.pallas_call(
        join_kernel,
        grid=(count // group,),
        out_shape=jax.ShapeDtypeStruct((rows, count * rows), jnp.float32),
        in_specs=[tile, tile],
        out_specs=pl.BlockSpec((rows, group * rows), lambda i: (0, i)),
        compiler_params=pltpu.CompilerParams(vmem_limit_bytes=32 * 2**20),
        name="join",
    )(straight, mirrored)


def shards(amplitudes, factors):
    rows = amplitudes.shape[0]
    block = factors.shape[0]
    half = block // 2
    core = lax.axis_index("c")
    parity = lax.axis_index("x") & 1

    def place(piece):
        first = parity if piece[0] == "a" else 1 - parity
        z = lax.axis_index("zl") ^ int(piece[1])
        y = (lax.axis_index("y") + (2 * core - 1) * int(piece[2])) & 3
        return 4 * z + y, first * half

    pieces = {
        "a00": lax.dynamic_slice_in_dim(factors, parity * half, half, 0),
        "b00": lax.dynamic_slice_in_dim(factors, (1 - parity) * half, half, 0),
    }

    def columns(wanted):
        return jnp.stack(
            [lax.dynamic_slice_in_dim(amplitudes, (2 * i + wanted) * block, block, 1) for i in range(8)]
        )

    theirs = lax.ppermute(columns(1 - core), ALL, CORES)
    both = jnp.concatenate([columns(core), theirs], axis=1)

    def multiply(name):
        at, offset = place(name)
        left = lax.dynamic_slice(both, (at, 0, offset), (1, 2 * rows, half))[0]
        return dot(left, pieces[name])

    def take(names, fitted):
        for name in names:
            term = multiply(name)
            fitted = term if fitted is None else fitted + term
        return fitted

    fitted = None
    ready = ["a00", "b00"]
    for moves in ROUNDS:
        sources = lax.optimization_barrier([pieces[source] for _, source, _ in moves])
        arrived = [lax.ppermute(value, ALL, route) for value, (route, _, _) in zip(sources, moves)]
        fitted = take(ready, fitted)
        arrived = lax.optimization_barrier(arrived)
        for value, (_, _, target) in zip(arrived, moves):
            pieces[target] = value
        ready = [target for _, _, target in moves]
    fitted = take(ready, fitted)

    swapped = lax.ppermute(fitted, ALL, CORES)
    fitted = fitted + jnp.concatenate([swapped[rows:], swapped[:rows]], axis=0)
    places = [place(name) for name in PIECES]
    group = block // rows
    mine_at = jnp.stack([(2 * at + core) * group + offset // rows for at, offset in places])
    theirs_at = jnp.stack([at * group + offset // rows for at, offset in places])
    owned, other = make_cycle(rows, mine_at, theirs_at, fitted, [pieces[name] for name in PIECES])
    other = lax.ppermute(other, ALL, CORES)
    owned = lax.dynamic_update_slice(
        owned.reshape(8, 2, group, rows, rows),
        other.reshape(8, 1, group, rows, rows),
        (0, 1 - core, 0, 0, 0),
    ).reshape(-1, rows, rows)
    moved = lax.all_to_all(owned, ALL, split_axis=0, concat_axis=0, tiled=True)
    return join(owned, moved)


def solution(mesh):
    mesh = Mesh(mesh.devices.reshape(SIZES), ALL)
    in_specs = (P(ALL, None), P(MEM, None))
    return jax.shard_map(
        shards, mesh=mesh, in_specs=in_specs, out_specs=P(ALL, None), check_vma=False
    )
```

```python
import functools

import jax
import jax.numpy as jnp
import numpy as np
from jax import lax
from jax.experimental import pallas as pl
from jax.experimental.pallas import tpu as pltpu
from jax.sharding import Mesh
from jax.sharding import PartitionSpec as P

SIZES = (2, 4, 2, 4, 2)
ALL = ("zh", "x", "zl", "y", "c")
MEM = ("zl", "y", "c")


def permutation(move):
    pairs = []
    for source in range(int(np.prod(SIZES))):
        zh, x, zl, y, c = (int(i) for i in np.unravel_index(source, SIZES))
        tx, ty, tz, tc = move(x, y, 2 * zh + zl, c)
        tx, ty, tz, tc = tx % 4, ty % 4, tz % 4, tc % 2
        pairs.append((source, int(np.ravel_multi_index((tz // 2, tx, tz % 2, ty, tc), SIZES))))
    return pairs


ALONG_X = permutation(lambda x, y, z, c: (x + 1 - 2 * c, y, z, c))
ALONG_Y = permutation(lambda x, y, z, c: (x, y + 1 - 2 * c, z, c))
ALONG_Z = permutation(lambda x, y, z, c: (x, y, z + 1 - 2 * c, c))
CORES = permutation(lambda x, y, z, c: (x, y, z, c + 1))

ROUNDS = (
    ((ALONG_Y, "a00", "a01"), (ALONG_Z, "a00", "a10")),
    ((ALONG_X, "a01", "b01"), (ALONG_Y, "a01", "a02"), (ALONG_Z, "b00", "b10")),
    ((ALONG_X, "a02", "b02"), (ALONG_Y, "a02", "a03"), (ALONG_Z, "a01", "a11")),
    ((ALONG_X, "a03", "b03"), (ALONG_Y, "b10", "b11"), (ALONG_Z, "a03", "a13")),
    ((ALONG_X, "a13", "b13"), (ALONG_Y, "b11", "b12"), (ALONG_Z, "a02", "a12")),
)


PIECES = ["a00", "b00"] + [target for moves in ROUNDS for _, _, target in moves]
SLOTS = 3
STREAMS = 2
NT = (((1,), (1,)), ((), ()))
NN = (((1,), (0,)), ((), ()))
LIMIT = pltpu.CompilerParams(vmem_limit_bytes=40 * 2**20)
BRIEF = pl.CostEstimate(flops=1000, bytes_accessed=1000, transcendentals=0)
ANYWHERE = pl.BlockSpec(memory_space=pl.ANY)
VECTOR = pl.BlockSpec(memory_space=pltpu.VMEM)
SCALAR = pl.BlockSpec(memory_space=pltpu.SMEM)


def parts(value):
    high = value.astype(jnp.bfloat16)
    return high, (value - high.astype(jnp.float32)).astype(jnp.bfloat16)


def product(a, b, numbers):
    multiply = functools.partial(
        lax.dot_general, dimension_numbers=numbers, preferred_element_type=jnp.float32
    )
    return (multiply(a[1], b[0]) + multiply(a[0], b[1])) + multiply(a[0], b[0])


def pick_kernel(half, at, source, out, sems):
    def copy(i):
        columns = pl.ds(pl.multiple_of(at[i] * half, 128), half)
        return pltpu.make_async_copy(source.at[:, columns], out.at[i], sems.at[i])

    for i in range(out.shape[0]):
        copy(i).start()
    for i in range(out.shape[0]):
        copy(i).wait()


def pick(amplitudes, at, half):
    count = at.shape[0]
    return pl.pallas_call(
        functools.partial(pick_kernel, half),
        out_shape=jax.ShapeDtypeStruct((count, amplitudes.shape[0], half), jnp.float32),
        in_specs=[SCALAR, ANYWHERE],
        out_specs=ANYWHERE,
        scratch_shapes=[pltpu.SemaphoreType.DMA((count,))],
        cost_estimate=BRIEF,
        compiler_params=LIMIT,
        name="pick",
    )(at, amplitudes)


def merge_kernel(at, pieces, whole_in, whole, sems):
    count = at.shape[0]
    size = pieces.shape[0] // count

    def copy(i):
        return pltpu.make_async_copy(
            pieces.at[pl.ds(i * size, size)], whole.at[pl.ds(at[i], size)], sems.at[i]
        )

    for i in range(count):
        copy(i).start()
    for i in range(count):
        copy(i).wait()


def merge(whole, pieces, at):
    return pl.pallas_call(
        merge_kernel,
        out_shape=jax.ShapeDtypeStruct(whole.shape, whole.dtype),
        in_specs=[SCALAR, ANYWHERE, ANYWHERE],
        out_specs=ANYWHERE,
        input_output_aliases={2: 0},
        scratch_shapes=[pltpu.SemaphoreType.DMA((at.shape[0],))],
        cost_estimate=BRIEF,
        compiler_params=LIMIT,
        name="merge",
    )(at, pieces, whole)


def fit_kernel(count, mine_at, theirs_at, amplitudes, theirs, before, *refs):
    pieces, (out, held, left, sems, left_sems) = refs[:count], refs[count:]
    rows = theirs.shape[1]
    half = theirs.shape[2]

    def fetch(i):
        columns = pl.ds(pl.multiple_of(mine_at[i] * half, 128), half)
        return (
            pltpu.make_async_copy(pieces[i], held.at[i], sems.at[i]),
            pltpu.make_async_copy(amplitudes.at[:, columns], left.at[i, :rows], left_sems.at[i, 0]),
            pltpu.make_async_copy(theirs.at[theirs_at[i]], left.at[i, rows:], left_sems.at[i, 1]),
        )

    for i in range(count):
        for copy in fetch(i):
            copy.start()
    total = before[...]
    for i in range(count):
        for copy in fetch(i):
            copy.wait()
        total = total + product(parts(left[i]), parts(held[i]), NN)
    out[...] = total


def fit(amplitudes, theirs, mine_at, theirs_at, pieces, before):
    count = len(pieces)
    half, depth = pieces[0].shape
    return pl.pallas_call(
        functools.partial(fit_kernel, count),
        out_shape=jax.ShapeDtypeStruct(before.shape, jnp.float32),
        in_specs=[SCALAR, SCALAR, ANYWHERE, ANYWHERE, VECTOR] + [ANYWHERE] * count,
        out_specs=VECTOR,
        scratch_shapes=[
            pltpu.VMEM((count, half, depth), jnp.float32),
            pltpu.VMEM((count, before.shape[0], half), jnp.float32),
            pltpu.SemaphoreType.DMA((count,)),
            pltpu.SemaphoreType.DMA((count, 2)),
        ],
        cost_estimate=BRIEF,
        compiler_params=LIMIT,
        name="fit",
    )(mine_at, theirs_at, amplitudes, theirs, before, *pieces)


def cycle_kernel(rows, first, based, chained, at, fitted, swapped, *refs):
    base, refs = refs[: 2 * based], refs[2 * based + chained :]
    scratch = 10 if based else 8
    pieces, refs = refs[:-scratch], refs[-scratch:]
    owned, other, high, low, held, tiles, in_sems, out_sems = refs[:8]
    count = len(pieces)
    half = pieces[0].shape[0]
    width = min(2 * rows, half)
    per_step = width // rows
    per_piece = half // rows

    def fetch(i):
        slot = i % SLOTS
        copies = [pltpu.make_async_copy(pieces[i], held.at[slot], in_sems.at[slot])]
        if based:
            before, before_sems = refs[8:]
            there = pl.ds((first + i) * per_piece, per_piece)
            copies += [
                pltpu.make_async_copy(base[k].at[there], before.at[slot, k], before_sems.at[slot, k])
                for k in range(2)
            ]
        return copies

    def drain(i):
        slot = i % 2
        return (
            pltpu.make_async_copy(
                tiles.at[slot, 0], owned.at[pl.ds(at[i], per_piece)], out_sems.at[slot, 0]
            ),
            pltpu.make_async_copy(
                tiles.at[slot, 1], other.at[pl.ds(i * per_piece, per_piece)], out_sems.at[slot, 1]
            ),
        )

    for i in range(min(SLOTS - 1, count)):
        for copy in fetch(i):
            copy.start()
    for who in range(2):
        mine = slice(who * rows, (who + 1) * rows)
        theirs = slice((1 - who) * rows, (2 - who) * rows)
        high[mine], low[mine] = parts(fitted[mine] + swapped[theirs])
    for i in range(count):
        if i + SLOTS - 1 < count:
            for copy in fetch(i + SLOTS - 1):
                copy.start()
        for copy in fetch(i):
            copy.wait()
        if i >= 2:
            for copy in drain(i - 2):
                copy.wait()
        for step in range(half // width):
            piece = parts(held[i % SLOTS, step * width : (step + 1) * width])
            total = product((high[...], low[...]), piece, NT)
            for k in range(per_step):
                tile = step * per_step + k
                for who in range(2):
                    value = total[who * rows : (who + 1) * rows, k * rows : (k + 1) * rows]
                    if based:
                        value = value + refs[8][i % SLOTS, who, tile]
                    tiles[i % 2, who, tile] = value
        for copy in drain(i):
            copy.start()
    for i in range(max(count - 2, 0), count):
        for copy in drain(i):
            copy.wait()


def make_cycle(rows, at, fitted, swapped, pieces, owned_tiles, first=0, base=(), owned=None):
    half, depth = pieces[0].shape
    tiles = (2, half // rows, rows, rows)
    scratch = [
        pltpu.VMEM(fitted.shape, jnp.bfloat16),
        pltpu.VMEM(fitted.shape, jnp.bfloat16),
        pltpu.VMEM((SLOTS, half, depth), jnp.float32),
        pltpu.VMEM((2,) + tiles, jnp.float32),
        pltpu.SemaphoreType.DMA((SLOTS,)),
        pltpu.SemaphoreType.DMA((2, 2)),
    ]
    if base:
        scratch += [pltpu.VMEM((SLOTS,) + tiles, jnp.float32), pltpu.SemaphoreType.DMA((SLOTS, 2))]
    chained = () if owned is None else (owned,)
    return pl.pallas_call(
        functools.partial(cycle_kernel, rows, first, bool(base), len(chained)),
        out_shape=(
            jax.ShapeDtypeStruct((owned_tiles, rows, rows), jnp.float32),
            jax.ShapeDtypeStruct((len(pieces) * half // rows, rows, rows), jnp.float32),
        ),
        in_specs=[SCALAR, VECTOR, VECTOR] + [ANYWHERE] * (len(base) + len(chained) + len(pieces)),
        out_specs=(ANYWHERE, ANYWHERE),
        input_output_aliases={3 + len(base): 0} if chained else {},
        scratch_shapes=scratch,
        cost_estimate=BRIEF,
        compiler_params=LIMIT,
        name="cycle",
    )(at, fitted, swapped, *base, *chained, *pieces)


def join_kernel(straight, mirrored, out):
    rows = straight.shape[1]
    for k in range(straight.shape[0]):
        out[:, k * rows : (k + 1) * rows] = straight[k] + mirrored[k].T


def join(straight, mirrored):
    count, rows, _ = straight.shape
    group = 16
    tile = pl.BlockSpec((group, rows, rows), lambda i: (i, 0, 0))
    return pl.pallas_call(
        join_kernel,
        grid=(count // group,),
        out_shape=jax.ShapeDtypeStruct((rows, count * rows), jnp.float32),
        in_specs=[tile, tile],
        out_specs=pl.BlockSpec((rows, group * rows), lambda i: (0, i)),
        compiler_params=pltpu.CompilerParams(vmem_limit_bytes=32 * 2**20),
        name="join",
    )(straight, mirrored)


def shards(amplitudes, factors):
    rows = amplitudes.shape[0]
    block = factors.shape[0]
    half = block // 2
    depth = factors.shape[1] // STREAMS
    group = block // rows
    size = half // rows
    core = lax.axis_index("c")
    parity = lax.axis_index("x") & 1

    def place(piece, who):
        z = lax.axis_index("zl") ^ int(piece[1])
        y = (lax.axis_index("y") + (2 * who - 1) * int(piece[2])) & 3
        return 4 * z + y, parity if piece[0] == "a" else 1 - parity

    def columns_at(names, who):
        found = [place(name, who) for name in names]
        return jnp.stack([2 * (2 * at + who) + which for at, which in found])

    def among(names):
        return jnp.stack([2 * at + which for at, which in [place(name, core) for name in names]])

    def tiles_at(names, who):
        return columns_at(names, who) * size

    def begin(name, stream):
        return lax.dynamic_slice(factors, (place(name, core)[1] * half, stream * depth), (half, depth))

    pieces = [{name: begin(name, k) for name in ("a00", "b00")} for k in range(STREAMS)]
    wanted = jnp.stack([2 * (2 * i + 1 - core) + which for i in range(8) for which in range(2)])

    def launch(stream, moves):
        sources = lax.optimization_barrier([pieces[stream][source] for _, source, _ in moves])
        return [lax.ppermute(value, ALL, route) for value, (route, _, _) in zip(sources, moves)]

    flying = [launch(k, ROUNDS[0]) for k in range(STREAMS)]
    theirs = lax.ppermute(pick(amplitudes, wanted, half), ALL, CORES)

    def multiply(stream, names, before):
        return fit(
            amplitudes,
            theirs,
            columns_at(names, core),
            among(names),
            [pieces[stream][name] for name in names],
            before,
        )

    fitted = [jnp.zeros((2 * rows, depth), jnp.float32) for _ in range(STREAMS)]
    base = None
    for number, moves in enumerate(ROUNDS):
        last = number + 1 == len(ROUNDS)
        for k in range(STREAMS):
            landed, theirs, fitted, base = lax.optimization_barrier((flying[k], theirs, fitted, base))
            for value, (_, _, target) in zip(landed, moves):
                pieces[k][target] = value
            if not last:
                flying[k] = launch(k, ROUNDS[number + 1])
            names = [target for _, _, target in moves]
            if number == 0:
                names = ["a00", "b00"] + names
            fitted[k] = multiply(k, names, fitted[k])
            if last:
                swapped = lax.ppermute(fitted[k], ALL, CORES)
                ordered = [pieces[k][name] for name in PIECES]
                if k == 0:
                    at = jnp.arange(len(PIECES), dtype=jnp.int32) * size
                    base = make_cycle(rows, at, fitted[k], swapped, ordered, 8 * group)

    owned = None
    others = []
    part = len(PIECES) // 2
    for first in range(0, len(PIECES), part):
        names = PIECES[first : first + part]
        owned, other = make_cycle(
            rows, tiles_at(names, core), fitted[-1], swapped, ordered[first : first + part],
            16 * group, first, base, owned,
        )
        others.append((names, lax.ppermute(other, ALL, CORES)))
    for names, other in others:
        owned = merge(owned, other, tiles_at(names, 1 - core))
    moved = lax.all_to_all(owned, ALL, split_axis=0, concat_axis=0, tiled=True)
    return join(owned, moved)


def solution(mesh):
    mesh = Mesh(mesh.devices.reshape(SIZES), ALL)
    in_specs = (P(ALL, None), P(MEM, None))
    return jax.shard_map(
        shards, mesh=mesh, in_specs=in_specs, out_specs=P(ALL, None), check_vma=False
    )
```

```python
import functools

import jax
import jax.numpy as jnp
import numpy as np
from jax import lax
from jax.experimental import pallas as pl
from jax.experimental.pallas import tpu as pltpu
from jax.sharding import Mesh
from jax.sharding import PartitionSpec as P

SIZES = (2, 4, 2, 4, 2)
ALL = ("zh", "x", "zl", "y", "c")
MEM = ("zl", "y", "c")


def permutation(move):
    pairs = []
    for source in range(int(np.prod(SIZES))):
        zh, x, zl, y, c = (int(i) for i in np.unravel_index(source, SIZES))
        tx, ty, tz, tc = move(x, y, 2 * zh + zl, c)
        tx, ty, tz, tc = tx % 4, ty % 4, tz % 4, tc % 2
        pairs.append((source, int(np.ravel_multi_index((tz // 2, tx, tz % 2, ty, tc), SIZES))))
    return pairs


ALONG_X = permutation(lambda x, y, z, c: (x + 1 - 2 * c, y, z, c))
ALONG_Y = permutation(lambda x, y, z, c: (x, y + 1 - 2 * c, z, c))
ALONG_Z = permutation(lambda x, y, z, c: (x, y, z + 1 - 2 * c, c))
CORES = permutation(lambda x, y, z, c: (x, y, z, c + 1))

ROUNDS = (
    ((ALONG_Y, "a00", "a01"), (ALONG_Z, "a00", "a10")),
    ((ALONG_X, "a01", "b01"), (ALONG_Y, "a01", "a02"), (ALONG_Z, "b00", "b10")),
    ((ALONG_X, "a02", "b02"), (ALONG_Y, "a02", "a03"), (ALONG_Z, "a01", "a11")),
    ((ALONG_X, "a03", "b03"), (ALONG_Y, "b10", "b11"), (ALONG_Z, "a03", "a13")),
    ((ALONG_X, "a13", "b13"), (ALONG_Y, "b11", "b12"), (ALONG_Z, "a02", "a12")),
)


PIECES = ["a00", "b00"] + [target for moves in ROUNDS for _, _, target in moves]
SLOTS = 3
STREAMS = 2
NT = (((1,), (1,)), ((), ()))
NN = (((1,), (0,)), ((), ()))
LIMIT = pltpu.CompilerParams(vmem_limit_bytes=40 * 2**20)
HALVES = 2
BRIEF = pl.CostEstimate(flops=1000, bytes_accessed=1000, transcendentals=0)
ANYWHERE = pl.BlockSpec(memory_space=pl.ANY)
VECTOR = pl.BlockSpec(memory_space=pltpu.VMEM)
SCALAR = pl.BlockSpec(memory_space=pltpu.SMEM)


def parts(value):
    high = value.astype(jnp.bfloat16)
    return high, (value - high.astype(jnp.float32)).astype(jnp.bfloat16)


def product(a, b, numbers):
    multiply = functools.partial(
        lax.dot_general, dimension_numbers=numbers, preferred_element_type=jnp.float32
    )
    return (multiply(a[1], b[0]) + multiply(a[0], b[1])) + multiply(a[0], b[0])


def copy_kernel(at, source, *refs):
    refs[-1][...] = source[...].reshape(refs[-1].shape)


def pick(amplitudes, at, half):
    count = at.shape[0]
    rows = amplitudes.shape[0]
    return pl.pallas_call(
        copy_kernel,
        grid_spec=pltpu.PrefetchScalarGridSpec(
            num_scalar_prefetch=1,
            grid=(count,),
            in_specs=[pl.BlockSpec((rows, half), lambda i, at: (0, at[i]))],
            out_specs=pl.BlockSpec((1, rows, half), lambda i, at: (i, 0, 0)),
        ),
        out_shape=jax.ShapeDtypeStruct((count, rows, half), jnp.float32),
        cost_estimate=BRIEF,
        compiler_params=LIMIT,
        name="pick",
    )(at, amplitudes)


def merge(whole, pieces, at):
    count = at.shape[0]
    block = (pieces.shape[0] // count,) + pieces.shape[1:]
    return pl.pallas_call(
        copy_kernel,
        grid_spec=pltpu.PrefetchScalarGridSpec(
            num_scalar_prefetch=1,
            grid=(count,),
            in_specs=[pl.BlockSpec(block, lambda i, at: (i, 0, 0)), ANYWHERE],
            out_specs=pl.BlockSpec(block, lambda i, at: (at[i], 0, 0)),
        ),
        out_shape=jax.ShapeDtypeStruct(whole.shape, whole.dtype),
        input_output_aliases={2: 0},
        cost_estimate=BRIEF,
        compiler_params=LIMIT,
        name="merge",
    )(at, pieces, whole)


def fit_kernel(count, mine_at, theirs_at, amplitudes, theirs, before, *refs):
    pieces, (out, held, left, sems, left_sems) = refs[:count], refs[count:]
    rows = theirs.shape[1]
    half = theirs.shape[2]

    def fetch(i):
        columns = pl.ds(pl.multiple_of(mine_at[i] * half, 128), half)
        return (
            pltpu.make_async_copy(pieces[i], held.at[i], sems.at[i]),
            pltpu.make_async_copy(amplitudes.at[:, columns], left.at[i, :rows], left_sems.at[i, 0]),
            pltpu.make_async_copy(theirs.at[theirs_at[i]], left.at[i, rows:], left_sems.at[i, 1]),
        )

    for i in range(count):
        for copy in fetch(i):
            copy.start()
    total = before[...]
    for i in range(count):
        for copy in fetch(i):
            copy.wait()
        total = total + product(parts(left[i]), parts(held[i]), NN)
    out[...] = total


def fit(amplitudes, theirs, mine_at, theirs_at, pieces, before):
    count = len(pieces)
    half, depth = pieces[0].shape
    return pl.pallas_call(
        functools.partial(fit_kernel, count),
        out_shape=jax.ShapeDtypeStruct(before.shape, jnp.float32),
        in_specs=[SCALAR, SCALAR, ANYWHERE, ANYWHERE, VECTOR] + [ANYWHERE] * count,
        out_specs=VECTOR,
        scratch_shapes=[
            pltpu.VMEM((count, half, depth), jnp.float32),
            pltpu.VMEM((count, before.shape[0], half), jnp.float32),
            pltpu.SemaphoreType.DMA((count,)),
            pltpu.SemaphoreType.DMA((count, 2)),
        ],
        cost_estimate=BRIEF,
        compiler_params=LIMIT,
        name="fit",
    )(mine_at, theirs_at, amplitudes, theirs, before, *pieces)


def cycle_kernel(rows, steps, based, at, fitted, swapped, *refs):
    base, refs = (refs[0], refs[1:]) if based else (None, refs)
    scratch = 10 if based else 7
    pieces, refs = refs[:-scratch], refs[-scratch:]
    outs, refs = refs[: 1 + based], refs[1 + based :]
    high, low, held, sums, in_sems, out_sems = refs[:6]
    targets = pieces[0].shape[0] // rows
    width = rows // HALVES

    def fetch(n):
        i, part = steps[n]
        slot = n % SLOTS
        copies = [
            pltpu.make_async_copy(
                pieces[i].at[pl.ds(t * rows + part * width, width)],
                held.at[slot, pl.ds(t * width, width)],
                in_sems.at[slot, t],
            )
            for t in range(targets)
        ]
        if based:
            before, before_sems = refs[6:]
            copies.append(
                pltpu.make_async_copy(base.at[i * HALVES + part], before.at[slot], before_sems.at[slot])
            )
        return copies

    def drain(n):
        slot = n % 2
        if not based:
            return [pltpu.make_async_copy(sums.at[slot], outs[0].at[n], out_sems.at[slot, 0])]
        i = steps[n][0]
        places = (pl.ds(at[i] * targets, targets), pl.ds(n * targets, targets))
        return [
            pltpu.make_async_copy(sums.at[slot, k], outs[k].at[places[k]], out_sems.at[slot, k])
            for k in range(2)
        ]

    for n in range(min(SLOTS - 1, len(steps))):
        for copy in fetch(n):
            copy.start()
    for who in range(2):
        mine = slice(who * rows, (who + 1) * rows)
        theirs = slice((1 - who) * rows, (2 - who) * rows)
        high[mine], low[mine] = parts(fitted[mine] + swapped[theirs])
    for n in range(len(steps)):
        if n + SLOTS - 1 < len(steps):
            for copy in fetch(n + SLOTS - 1):
                copy.start()
        for copy in fetch(n):
            copy.wait()
        if n >= 2:
            for copy in drain(n - 2):
                copy.wait()
        total = product(parts(held[n % SLOTS]), (high[...], low[...]), NT)
        if based:
            total = total + refs[6][n % SLOTS]
            for k in range(2):
                for t in range(targets):
                    sums[n % 2, k, t] = total[t * width : (t + 1) * width, k * rows : (k + 1) * rows]
        else:
            sums[n % 2] = total
        for copy in drain(n):
            copy.start()
    for n in range(max(len(steps) - 2, 0), len(steps)):
        for copy in drain(n):
            copy.wait()


def make_cycle(rows, at, fitted, swapped, pieces, steps, base=None):
    half, depth = pieces[0].shape
    targets = half // rows
    width = rows // HALVES
    scratch = [
        pltpu.VMEM(fitted.shape, jnp.bfloat16),
        pltpu.VMEM(fitted.shape, jnp.bfloat16),
        pltpu.VMEM((SLOTS, targets * width, depth), jnp.float32),
    ]
    if base is None:
        out = jax.ShapeDtypeStruct((len(steps), targets * width, 2 * rows), jnp.float32)
        outs, out_specs, more = out, ANYWHERE, []
        scratch += [pltpu.VMEM((2,) + out.shape[1:], jnp.float32)]
    else:
        outs = (
            jax.ShapeDtypeStruct((2 * len(steps) * targets, width, rows), jnp.float32),
            jax.ShapeDtypeStruct((len(steps) * targets, width, rows), jnp.float32),
        )
        out_specs = (ANYWHERE, ANYWHERE)
        more = [
            pltpu.VMEM((SLOTS, targets * width, 2 * rows), jnp.float32),
            pltpu.SemaphoreType.DMA((SLOTS,)),
        ]
        scratch += [pltpu.VMEM((2, 2, targets, width, rows), jnp.float32)]
    scratch += [pltpu.SemaphoreType.DMA((SLOTS, targets)), pltpu.SemaphoreType.DMA((2, 2))] + more
    bases = [] if base is None else [base]
    return pl.pallas_call(
        functools.partial(cycle_kernel, rows, steps, len(bases)),
        out_shape=outs,
        in_specs=[SCALAR, VECTOR, VECTOR] + [ANYWHERE] * (len(bases) + len(pieces)),
        out_specs=out_specs,
        scratch_shapes=scratch,
        cost_estimate=BRIEF,
        compiler_params=LIMIT,
        name="cycle",
    )(at, fitted, swapped, *bases, *pieces)


def join_kernel(*refs):
    owned, moved, out = refs[:HALVES], refs[HALVES:-1], refs[-1]
    rows = owned[0].shape[2]
    for k in range(owned[0].shape[0]):
        straight = jnp.concatenate([ref[k] for ref in owned], axis=0).T
        mirrored = jnp.concatenate([ref[k] for ref in moved], axis=0)
        out[:, k * rows : (k + 1) * rows] = straight + mirrored


def join(owned, moved):
    count, width, rows = owned[0].shape
    group = 16
    tile = pl.BlockSpec((group, width, rows), lambda i: (i, 0, 0))
    return pl.pallas_call(
        join_kernel,
        grid=(count // group,),
        out_shape=jax.ShapeDtypeStruct((rows, count * rows), jnp.float32),
        in_specs=[tile] * (2 * HALVES),
        out_specs=pl.BlockSpec((rows, group * rows), lambda i: (0, i)),
        compiler_params=LIMIT,
        name="join",
    )(*owned, *moved)


def shards(amplitudes, factors):
    rows = amplitudes.shape[0]
    block = factors.shape[0]
    half = block // 2
    depth = factors.shape[1] // STREAMS
    core = lax.axis_index("c")
    parity = lax.axis_index("x") & 1

    def place(piece, who):
        z = lax.axis_index("zl") ^ int(piece[1])
        y = (lax.axis_index("y") + (2 * who - 1) * int(piece[2])) & 3
        return 4 * z + y, parity if piece[0] == "a" else 1 - parity

    def columns_at(names, who):
        found = [place(name, who) for name in names]
        return jnp.stack([2 * (2 * at + who) + which for at, which in found])

    def among(names):
        return jnp.stack([2 * at + which for at, which in [place(name, core) for name in names]])

    def begin(source, name, stream):
        return lax.dynamic_slice(source, (place(name, core)[1] * half, stream * depth), (half, depth))

    pieces = [{"a00": begin(factors, "a00", 0)}, {}]
    pieces[0]["a00"], factors = lax.optimization_barrier((pieces[0]["a00"], factors))
    pieces[1]["a00"] = begin(factors, "a00", 1)
    pieces[1]["a00"], factors, early = lax.optimization_barrier((pieces[1]["a00"], factors, amplitudes))
    for k in range(STREAMS):
        pieces[k]["b00"] = begin(factors, "b00", k)
    wanted = jnp.stack([2 * (2 * i + 1 - core) + which for i in range(8) for which in range(2)])

    def launch(stream, moves):
        sources = lax.optimization_barrier([pieces[stream][source] for _, source, _ in moves])
        return [lax.ppermute(value, ALL, route) for value, (route, _, _) in zip(sources, moves)]

    flying = [launch(k, ROUNDS[0]) for k in range(STREAMS)]
    theirs = lax.ppermute(pick(early, wanted, half), ALL, CORES)

    def multiply(stream, names, before):
        return fit(
            amplitudes,
            theirs,
            columns_at(names, core),
            among(names),
            [pieces[stream][name] for name in names],
            before,
        )

    mine_at = columns_at(PIECES, core)
    theirs_at = columns_at(PIECES, 1 - core)
    fitted = [jnp.zeros((2 * rows, depth), jnp.float32) for _ in range(STREAMS)]
    base = None
    for number, moves in enumerate(ROUNDS):
        last = number + 1 == len(ROUNDS)
        for k in range(STREAMS):
            landed, theirs, fitted, base = lax.optimization_barrier((flying[k], theirs, fitted, base))
            for value, (_, _, target) in zip(landed, moves):
                pieces[k][target] = value
            if not last:
                flying[k] = launch(k, ROUNDS[number + 1])
            names = [target for _, _, target in moves]
            if number == 0:
                names = ["a00", "b00"] + names
            fitted[k] = multiply(k, names, fitted[k])
            if last:
                swapped = lax.ppermute(fitted[k], ALL, CORES)
                ordered = [pieces[k][name] for name in PIECES]
                if k == 0:
                    steps = [(i, part) for i in range(len(PIECES)) for part in range(HALVES)]
                    base = make_cycle(rows, mine_at, fitted[k], swapped, ordered, steps)

    sums = fitted[-1]
    owned, moved = [], []
    for part in range(HALVES):
        steps = [(i, part) for i in range(len(PIECES))]
        tiles, other = make_cycle(rows, mine_at, sums, swapped, ordered, steps, base)
        tiles = merge(tiles, lax.ppermute(other, ALL, CORES), theirs_at)
        tiles, sums = lax.optimization_barrier((tiles, sums))
        owned.append(tiles)
        moved.append(lax.all_to_all(tiles, ALL, split_axis=0, concat_axis=0, tiled=True))
    return join(owned, moved)


def solution(mesh):
    mesh = Mesh(mesh.devices.reshape(SIZES), ALL)
    in_specs = (P(ALL, None), P(MEM, None))
    return jax.shard_map(
        shards, mesh=mesh, in_specs=in_specs, out_specs=P(ALL, None), check_vma=False
    )
```
